768 devices in a mesh: lon: 96 (over z, y_hi, x), colat: 8 (over y_lo, core).
Axes of the slice: x: 4, y: 8 (y_hi: 2, y_lo: 4; y = y_hi * 4 + y_lo), z: 12, core: 2. Of those that a mesh axis runs over, the one named last changes fastest.
Arguments:
- pattern: bfloat16 [192, 2, 128, 384], P('lon', None, 'colat'), may hold values from -6 to 6
- phi_filter: bfloat16 [384, 384], replicated, may hold values from -0.3125 to 0.3125
- trans_table: float32 [316, 2, 128, 384], P(None, None, None, 'lon'), may hold values from -0.66 to 0.66
- partners: int32 [192, 40], replicated, may hold values from 0 to 191
- op_index: int32 [192, 40], replicated, may hold values from 0 to 315
- anter_weight: float32 [17, 128], P(None, 'colat'), may hold values from -1.5 to 1.5
- return_boxes: int32 [96, 5], replicated, may hold values from 0 to 191, as said below
- return_count: int32 [96], P('lon'), may hold values from 1 to 5, as said below
- leaf_weight: bfloat16 [2, 128, 384, 256], P(None, 'colat'), may hold values from -0.01953125 to 0.01953125
Outputs:
- leaf_field: float32 [96, 5, 256], P('lon', None, 'colat')
The draws below stay inside these ranges and needn't reach their ends.
Inputs may be any that keep to these rules, and one draw needn't show every extreme that they name: `return_boxes`: every box appears exactly once among the first return_count[j] entries of row j over all j; padded entries are 0. Some leaf owner receives exactly 5 boxes. `return_count`: the counts sum to 192.
All inputs are finite; a program needn't handle non-finite values.
Results may differ from the reference program's by a relative error of at most 0.0041.
Values may be sent and summed in bfloat16 or wider, within the bound.
A program may use at most 32 MiB of HBM per device.

```python
import jax
import jax.numpy as jnp
from jax import lax

BOX_DEV = 2
THETA = 128
PHI = 384
PARTNERS = 40
NOPS = 316
EDGE = 8
U = 256
BOXES = 192
RMAX = 5
N_LON = 96


def return_plan(key):
    order_devices = jax.random.permutation(jax.random.fold_in(key, 11), N_LON)
    ranking = jnp.argsort(order_devices).astype(jnp.int32)
    quarter = N_LON // 8
    delta = jnp.where(ranking < quarter, 3, jnp.where(ranking < 4 * quarter, -1, 0))
    counts = (BOX_DEV + delta).astype(jnp.int32)
    order_boxes = jax.random.permutation(jax.random.fold_in(key, 12), BOXES).astype(jnp.int32)
    offsets = jnp.cumsum(counts) - counts
    within = jnp.arange(RMAX, dtype=jnp.int32)[None, :]
    slots = jnp.clip(offsets[:, None] + within, 0, BOXES - 1)
    valid = within < counts[:, None]
    boxes = jnp.where(valid, order_boxes[slots], 0).astype(jnp.int32)
    return (boxes, counts)


def draw_return_boxes(key, part):
    return return_plan(key)[0]


def draw_return_count(key, part):
    return return_plan(key)[1]


def touch_ends(values, rng, smallest, high):
    extent = values.shape
    spot = [jax.random.randint(jax.random.fold_in(rng, axis), (), 0, extent[axis]) for axis in range(len(extent))]
    values = values.at[tuple(spot)].set(smallest)
    longest = extent.index(max(extent))
    spot[longest] = (spot[longest] + 1) % extent[longest]
    return values.at[tuple(spot)].set(high)


def shard_levels(own_key, extent, shards, smallest, high):
    def one(position, blocks):
        steps = jax.random.uniform(jax.random.fold_in(jax.random.fold_in(own_key, 6), position), (blocks,), jnp.float32, smallest / len(shards), high / len(shards))
        return jnp.repeat(jnp.exp(steps), extent[position] // blocks).reshape((-1,) + (1,) * (len(extent) - position - 1))

    factor_of = one(*shards[0])
    for cut in shards[1:]:
        factor_of = factor_of * one(*cut)
    return factor_of


def normal_values(stream_key, extent, deviation, bound, cuts=(), kind=jnp.bfloat16):
    gain = shard_levels(stream_key, extent, cuts, -0.22, 0.18) if cuts else 1.0
    values = jax.random.normal(stream_key, extent, jnp.float32) * deviation * gain
    return jnp.minimum(jnp.maximum(values, -bound), bound).astype(kind)


def setup_inputs(seed: int = 0) -> dict:
    key_of = jax.random.split(jax.random.key(seed), 10)
    return {
        "pattern": normal_values(key_of[0], (BOXES, 2, THETA, PHI), 1.0, 6.0, ((0, 96), (2, 8))),
        "phi_filter": normal_values(key_of[1], (PHI, PHI), PHI ** -0.5, 0.3125),
        "trans_table": normal_values(key_of[2], (NOPS, 2, THETA, PHI), 0.11, 0.66, ((3, 96),), jnp.float32),
        "partners": touch_ends(jax.random.randint(key_of[3], (BOXES, PARTNERS), 0, BOXES), jax.random.fold_in(key_of[3], 1), 0, BOXES - 1).astype(jnp.int32),
        "op_index": touch_ends(jax.random.randint(key_of[4], (BOXES, PARTNERS), 0, NOPS), jax.random.fold_in(key_of[4], 1), 0, NOPS - 1).astype(jnp.int32),
        "anter_weight": normal_values(key_of[5], (2 * EDGE + 1, THETA), 0.25, 1.5, ((1, 8),), jnp.float32),
        "return_boxes": draw_return_boxes(jax.random.fold_in(key_of[9], 71), 0),
        "return_count": draw_return_count(jax.random.fold_in(key_of[9], 71), 0),
        "leaf_weight": normal_values(key_of[8], (2, THETA, PHI, U), (2 * THETA * PHI) ** -0.5, 0.01953125, ((1, 8),)),
    }


def reference(pattern, phi_filter, trans_table, partners, op_index, anter_weight, return_boxes, return_count, leaf_weight):
    filtered = jnp.dot(pattern.reshape(-1, PHI), phi_filter, preferred_element_type=jnp.float32)
    filtered = filtered.reshape(BOXES, 2, THETA, PHI).astype(jnp.bfloat16)

    def add_partner(index, total):
        source = filtered[partners[:, index]].astype(jnp.float32)
        factor = trans_table[op_index[:, index]]
        real_part = factor[:, 0] * source[:, 0] - factor[:, 1] * source[:, 1]
        imag_part = factor[:, 0] * source[:, 1] + factor[:, 1] * source[:, 0]
        return total + jnp.stack([real_part, imag_part], axis=1)

    translated = lax.fori_loop(0, PARTNERS, add_partner, jnp.zeros((BOXES, 2, THETA, PHI), jnp.float32))
    padded = jnp.pad(translated, ((0, 0), (0, 0), (EDGE, EDGE), (0, 0)))
    anter = jnp.zeros((BOXES, 2, THETA, PHI), jnp.float32)
    for shift in range(2 * EDGE + 1):
        anter = anter + anter_weight[shift][None, None, :, None] * padded[:, :, shift:shift + THETA, :]
    anter = anter.astype(jnp.bfloat16)
    rows = anter[return_boxes.reshape(-1)].reshape(N_LON * RMAX, 2 * THETA * PHI)
    leaf = jnp.dot(rows, leaf_weight.reshape(2 * THETA * PHI, U), preferred_element_type=jnp.float32)
    leaf = leaf.reshape(N_LON, RMAX, U)
    valid = jnp.arange(RMAX, dtype=jnp.int32)[None, :] < return_count[:, None]
    return jnp.where(valid[:, :, None], leaf, jnp.float32(0.0))
```

```python
import functools

import jax
import jax.numpy as jnp
from jax import lax
from jax.experimental import pallas as pl
from jax.experimental.pallas import tpu as pltpu
from jax.sharding import PartitionSpec as P

F32, BF16, I32 = jnp.float32, jnp.bfloat16, jnp.int32
MESH = pl.DeviceIdType.MESH
EDGE = 8
UC = 32
RS_ROWS = 48


def dot(a, b):
    return jnp.dot(a, b, preferred_element_type=F32)


def dot_nt(a, b):
    return lax.dot_general(a, b, (((1,), (1,)), ((), ())), preferred_element_type=F32)


def split(x):
    hi = x.astype(BF16)
    return hi, (x - hi.astype(F32)).astype(BF16)


def iota(shape, axis):
    return lax.broadcasted_iota(I32, shape, axis)


def ones_where(mask):
    return jnp.where(mask, 1.0, 0.0).astype(F32)


def band(taps, first, offset, rows, phi_lane):
    along = jnp.concatenate([taps, jnp.zeros((112, 128), F32)], axis=0).T
    t_out = iota((128, 128), 0) & 15
    shift = t_out - (iota((128, 128), 1) + offset) + EDGE
    mixed = jnp.zeros((128, 128), F32)
    for s in range(2 * EDGE + 1):
        mixed = mixed + jnp.where(shift == s, along[s : s + 1, :], 0.0)
    wide = 32 * rows
    lane = iota((128, wide), 1)
    spread = ones_where(iota((128, wide), 0) == ((lane >> 4) & (rows - 1)) + first).astype(BF16)
    row = iota((128, wide), 0)
    same = (row >> 6) == (lane // (16 * rows))
    keep = ones_where(same & ((lane & 15) == phi_lane + ((row >> 4) & 3)))
    hi, lo = split(mixed)
    return (dot(hi, spread) * keep).astype(BF16), (dot(lo, spread) * keep).astype(BF16)


def kernel(
    lon,
    colat,
    pattern,
    phi_filter,
    partners,
    ops,
    taps,
    returns,
    count,
    table,
    weight,
    out,
    outbox,
    inbox,
    ybuf,
    tab,
    tcat_hi,
    tcat_lo,
    tab_t,
    src,
    rcat,
    factors,
    picks,
    lw_own,
    lw_prev,
    lw_next,
    tapsbox,
    acc,
    rs_out,
    rs_in,
    gbd_hi,
    gbd_lo,
    ohret,
    outbox2,
    inbox2,
    local_sem,
    halo_send,
    halo_recv,
    a_send,
    a_recv,
    rs_send,
    rs_recv,
    b_send,
    b_recv,
):
    i = lax.axis_index("lon")
    k = lax.axis_index("colat")
    prev_k = lax.rem(k + colat - 1, colat)
    next_k = lax.rem(k + 1, colat)
    nops8 = table.shape[0]
    theta = table.shape[1]
    npart, nbox = partners.shape

    barrier = pltpu.get_barrier_semaphore()

    def greet_lon(s, carry):
        pl.semaphore_signal(barrier, inc=1, device_id={"lon": lax.rem(i + s, lon)}, device_id_type=MESH)
        return carry

    def greet_colat(s, carry):
        pl.semaphore_signal(barrier, inc=1, device_id={"colat": lax.rem(k + s, colat)}, device_id_type=MESH)
        return carry

    lax.fori_loop(1, lon, greet_lon, 0)
    lax.fori_loop(1, colat, greet_colat, 0)

    block = pl.multiple_of(lax.div(i, 4) * 16, 16)
    load_table = pltpu.make_async_copy(table, tab.at[pl.ds(0, nops8)], local_sem.at[0])
    load_table.start()
    load_lw = pltpu.make_async_copy(weight.at[:, :, pl.ds(block, 16), :], lw_own, local_sem.at[1])
    load_lw.start()

    rows2 = jnp.concatenate([pattern[...], pattern[...]], axis=0)
    filtered = dot(rows2, phi_filter[...]).astype(BF16).astype(F32)
    ybuf[...] = filtered.T
    left = iota((lon, 128), 1) < 64
    for h in range(2):
        low = ybuf[pl.ds(2 * h, lon, stride=4), :]
        high = ybuf[pl.ds(2 * h + 1, lon, stride=4), :]
        outbox[:, h, :] = jnp.where(left, low, high)
    tapsbox[0, :, 0:17] = taps[...]

    pl.semaphore_wait(barrier, lon + colat - 2)

    def send_a(s, carry):
        to = lax.rem(i + s, lon)
        pltpu.make_async_remote_copy(
            src_ref=outbox.at[to],
            dst_ref=inbox.at[i],
            send_sem=a_send,
            recv_sem=a_recv,
            device_id={"lon": to},
            device_id_type=MESH,
        ).start()
        return carry

    lax.fori_loop(1, lon, send_a, 0)
    keep_a = pltpu.make_async_copy(outbox.at[i], inbox.at[i], local_sem.at[2])
    keep_a.start()

    halos = []
    for n, (part, first, dst, to) in enumerate(((lw_prev, 8, 1, next_k), (lw_next, 0, 2, prev_k))):
        halos.append(
            pltpu.make_async_remote_copy(
                src_ref=weight.at[:, pl.ds(first, 8), pl.ds(block, 16), :],
                dst_ref=part,
                send_sem=halo_send.at[2 * n],
                recv_sem=halo_recv.at[2 * n],
                device_id={"colat": to},
                device_id_type=MESH,
            )
        )
        halos.append(
            pltpu.make_async_remote_copy(
                src_ref=tapsbox.at[0],
                dst_ref=tapsbox.at[dst],
                send_sem=halo_send.at[2 * n + 1],
                recv_sem=halo_recv.at[2 * n + 1],
                device_id={"colat": to},
                device_id_type=MESH,
            )
        )
    for copy in halos:
        copy.start()

    tab[pl.ds(nops8, tab.shape[0] - nops8), :] = jnp.zeros((tab.shape[0] - nops8, theta), F32)
    load_table.wait()
    ops_pad = tab.shape[0] // 8
    for part in range(8):
        hi, lo = split(tab[pl.ds(part, ops_pad, stride=8), :])
        tcat_hi[:, part * theta : (part + 1) * theta] = hi
        tcat_lo[:, part * theta : (part + 1) * theta] = lo
    n = iota((256, 8 * theta), 0)
    x = iota((256, 8 * theta), 1)
    match = (lax.rem(x, theta) == 16 * k + (n & 15)) & (lax.div(x, theta) == (n >> 7) * 4 + ((n >> 4) & 3))
    sign = jnp.where(((n >> 7) == 1) & (((n >> 6) & 1) == 0), -1.0, 1.0)
    choose = jnp.where(match, sign, 0.0).astype(BF16)
    tab_t[:, :ops_pad] = dot_nt(choose, tcat_hi[...]).astype(BF16)
    tab_t[:, ops_pad:] = dot_nt(choose, tcat_lo[...]).astype(BF16)

    def gather_factors(p, carry):
        hot = ones_where(iota((ops_pad, nbox), 0) == ops[pl.ds(p, 1), :]).astype(BF16)
        factors[p] = dot(tab_t[...], jnp.concatenate([hot, hot], axis=0))
        partner = partners[pl.ds(p, 1), :]
        row = (partner & 1) * 128 + (partner >> 1)
        picks[p] = ones_where(iota((256, nbox), 0) == row).astype(BF16)
        return carry

    lax.fori_loop(0, npart, gather_factors, 0)

    load_lw.wait()
    for copy in halos:
        copy.wait_recv()
    phi_lane = 4 * lax.rem(i, 4)
    users = weight.shape[3]
    folded = jnp.zeros((128, users), F32)
    for part, (box, first, offset, rows) in enumerate(
        ((lw_own, 0, 0, 16), (lw_prev, 8, -16, 8), (lw_next, 0, 16, 8))
    ):
        hi, lo = band(tapsbox[part], first, offset, rows, phi_lane)
        leaf = box[...].reshape(32 * rows, users)
        term = dot(hi, leaf) + dot(lo, leaf)
        if part == 1:
            term = jnp.where(k > 0, term, 0.0)
        if part == 2:
            term = jnp.where(k < colat - 1, term, 0.0)
        folded = folded + term
    fold_hi, fold_lo = split(folded.T)
    fold = jnp.concatenate([fold_hi, fold_hi, fold_lo], axis=1)

    gbd_hi[...] = jnp.zeros(gbd_hi.shape, BF16)
    gbd_lo[...] = jnp.zeros(gbd_lo.shape, BF16)
    rcat[...] = jnp.zeros(rcat.shape, BF16)
    slots = returns.shape[0]
    listed = jnp.concatenate([returns[...], jnp.zeros((slots, 128 - lon), I32)], axis=1)
    listed = jnp.concatenate([listed, jnp.zeros((128 - slots, 128), I32)], axis=0).astype(F32).T
    for r in range(slots):
        column = listed[:lon, r : r + 1].astype(I32)
        ohret[:, r * 256 : (r + 1) * 256] = ones_where(iota((lon, 256), 1) == column).astype(BF16)

    xn = iota((512, 256), 0)
    xk = iota((512, 256), 1)
    phi = ((xk >> 7) & 1) * 2 + ((xk >> 6) & 1)
    part_in = ((xn >> 6) & 1) ^ ((xn >> 7) & 1)
    place = (
        ((xk & 15) == (xn & 15))
        & (phi == ((xn >> 4) & 3))
        & (((xk >> 4) & 1) == part_in)
        & (((xk >> 5) & 1) == (xn >> 8))
    )
    place = ones_where(place).astype(BF16)
    keep_a.wait()
    pltpu.make_async_copy(inbox.at[pl.ds(0, lon - 1)], inbox.at[pl.ds(0, lon - 1)], a_recv).wait()
    rcat[:lon, :] = jnp.concatenate([inbox[:, 0, :], inbox[:, 1, :]], axis=1).astype(BF16)
    wide = dot_nt(place, rcat[...]).astype(BF16)
    src[:, :128] = wide[:256]
    src[:, 128:] = wide[256:]

    acc[...] = jnp.zeros(acc.shape, F32)

    def translate(g, carry):
        term = jnp.zeros(acc.shape, F32)
        for q in range(4):
            term = term + dot(src[...], picks[4 * g + q]) * factors[4 * g + q]
        acc[...] += term
        return carry

    lax.fori_loop(0, npart // 4, translate, 0)
    t_hi, t_lo = split(acc[:128, :] + acc[128:, :])
    partial = dot(fold, jnp.concatenate([t_hi, t_lo, t_hi], axis=0))

    for c in range(colat):
        rs_out[c, :UC, :] = partial[c * UC : (c + 1) * UC, :128]
        rs_out[c, UC:, :64] = partial[c * UC : c * UC + 16, 128:192]
        rs_out[c, UC:, 64:] = partial[c * UC + 16 : (c + 1) * UC, 128:192]

    def send_rs(s, carry):
        to = lax.rem(k + s, colat)
        pltpu.make_async_remote_copy(
            src_ref=rs_out.at[to],
            dst_ref=rs_in.at[k],
            send_sem=rs_send,
            recv_sem=rs_recv,
            device_id={"colat": to},
            device_id_type=MESH,
        ).start()
        return carry

    lax.fori_loop(1, colat, send_rs, 0)
    keep_rs = pltpu.make_async_copy(rs_out.at[k], rs_in.at[k], local_sem.at[3])
    keep_rs.start()
    keep_rs.wait()
    pltpu.make_async_copy(rs_in.at[pl.ds(0, colat - 1)], rs_in.at[pl.ds(0, colat - 1)], rs_recv).wait()
    total = rs_in[0]
    for c in range(1, colat):
        total = total + rs_in[c]
    tail = jnp.concatenate([total[UC:, :], pltpu.roll(total[UC:, :], 64, 1)], axis=0)
    tail = jnp.where(iota((UC, 128), 1) < 64, tail, 0.0)
    g_hi, g_lo = split(jnp.concatenate([total[:UC, :], tail], axis=1))
    for r in range(4):
        gbd_hi[r * UC : (r + 1) * UC, r * 256 : (r + 1) * 256] = g_hi
        gbd_lo[r * UC : (r + 1) * UC, r * 256 : (r + 1) * 256] = g_lo
    outbox2[:, 0, :] = dot_nt(ohret[:, :1024], gbd_hi[...]) + dot_nt(ohret[:, :1024], gbd_lo[...])
    outbox2[:, 1, :] = dot_nt(ohret[:, 1024:], gbd_hi[:, :256]) + dot_nt(ohret[:, 1024:], gbd_lo[:, :256])

    def send_b(s, carry):
        to = lax.rem(i + s, lon)
        pltpu.make_async_remote_copy(
            src_ref=outbox2.at[to],
            dst_ref=inbox2.at[i],
            send_sem=b_send,
            recv_sem=b_recv,
            device_id={"lon": to},
            device_id_type=MESH,
        ).start()
        return carry

    lax.fori_loop(1, lon, send_b, 0)
    keep_b = pltpu.make_async_copy(outbox2.at[i], inbox2.at[i], local_sem.at[4])
    keep_b.start()
    keep_b.wait()
    pltpu.make_async_copy(inbox2.at[pl.ds(0, lon - 1)], inbox2.at[pl.ds(0, lon - 1)], b_recv).wait()
    field = jnp.sum(inbox2[...], axis=0)
    result = jnp.concatenate([field[0:1, r * UC : (r + 1) * UC] for r in range(4)] + [field[1:2, :UC]], axis=0)
    out[0] = jnp.where(iota((slots, UC), 0) < count[0], result, 0.0)

    for copy in halos:
        copy.wait_send()
    pltpu.make_async_copy(outbox.at[pl.ds(0, lon - 1)], outbox.at[pl.ds(0, lon - 1)], a_send).wait()
    pltpu.make_async_copy(rs_out.at[pl.ds(0, colat - 1)], rs_out.at[pl.ds(0, colat - 1)], rs_send).wait()
    pltpu.make_async_copy(outbox2.at[pl.ds(0, lon - 1)], outbox2.at[pl.ds(0, lon - 1)], b_send).wait()


def body(
    lon,
    colat,
    pattern,
    phi_filter,
    trans_table,
    partners,
    op_index,
    anter_weight,
    return_boxes,
    return_count,
    leaf_weight,
):
    nops, _, theta, _ = trans_table.shape
    npart, nbox = partners.shape[1], partners.shape[0]
    slots = return_boxes.shape[1]
    phi = phi_filter.shape[0]
    users = leaf_weight.shape[3]
    ops_pad = -(-nops // 128) * 128
    vmem, hbm = pl.BlockSpec(memory_space=pltpu.VMEM), pl.BlockSpec(memory_space=pl.ANY)
    smem = pl.BlockSpec(memory_space=pltpu.SMEM)
    return pl.pallas_call(
        functools.partial(kernel, lon, colat),
        out_shape=jax.ShapeDtypeStruct((1, slots, users // colat), F32),
        in_specs=[vmem, vmem, vmem, vmem, vmem, vmem, smem, hbm, hbm],
        out_specs=vmem,
        scratch_shapes=[
            pltpu.VMEM((lon, 2, 128), F32),
            pltpu.VMEM((lon, 2, 128), F32),
            pltpu.VMEM((phi, 128), F32),
            pltpu.VMEM((ops_pad * 8, theta), F32),
            pltpu.VMEM((ops_pad, 8 * theta), BF16),
            pltpu.VMEM((ops_pad, 8 * theta), BF16),
            pltpu.VMEM((256, 2 * ops_pad), BF16),
            pltpu.VMEM((256, 256), BF16),
            pltpu.VMEM((128, 256), BF16),
            pltpu.VMEM((npart, 256, nbox), F32),
            pltpu.VMEM((npart, 256, nbox), BF16),
            pltpu.VMEM((2, 16, 16, users), BF16),
            pltpu.VMEM((2, 8, 16, users), BF16),
            pltpu.VMEM((2, 8, 16, users), BF16),
            pltpu.VMEM((3, 16, 128), F32),
            pltpu.VMEM((256, nbox), F32),
            pltpu.VMEM((colat, RS_ROWS, 128), F32),
            pltpu.VMEM((colat, RS_ROWS, 128), F32),
            pltpu.VMEM((128, 1024), BF16),
            pltpu.VMEM((128, 1024), BF16),
            pltpu.VMEM((lon, slots * 256), BF16),
            pltpu.VMEM((lon, 2, 128), F32),
            pltpu.VMEM((lon, 2, 128), F32),
            pltpu.SemaphoreType.DMA((5,)),
            pltpu.SemaphoreType.DMA((4,)),
            pltpu.SemaphoreType.DMA((4,)),
            pltpu.SemaphoreType.DMA,
            pltpu.SemaphoreType.DMA,
            pltpu.SemaphoreType.DMA,
            pltpu.SemaphoreType.DMA,
            pltpu.SemaphoreType.DMA,
            pltpu.SemaphoreType.DMA,
        ],
        compiler_params=pltpu.CompilerParams(
            collective_id=0, has_side_effects=True, vmem_limit_bytes=60 * 1024 * 1024
        ),
        name="mlfma_pass",
    )(
        pattern.reshape(-1, phi),
        phi_filter,
        partners.T,
        op_index.T,
        anter_weight.T,
        return_boxes.T,
        return_count,
        trans_table.transpose(0, 1, 3, 2).reshape(nops * 8, theta),
        leaf_weight,
    )


def solution(mesh):
    in_specs = (
        P("lon", None, "colat", None),
        P(),
        P(None, None, None, "lon"),
        P(),
        P(),
        P(None, "colat"),
        P(),
        P("lon"),
        P(None, "colat", None, None),
    )
    out_specs = P("lon", None, "colat")
    run = functools.partial(body, mesh.shape["lon"], mesh.shape["colat"])
    return jax.shard_map(run, mesh=mesh, in_specs=in_specs, out_specs=out_specs, check_vma=False)
```

```python
import functools

import jax
import jax.numpy as jnp
from jax import lax
from jax.experimental import pallas as pl
from jax.experimental.pallas import tpu as pltpu
from jax.sharding import PartitionSpec as P

F32, BF16, I32 = jnp.float32, jnp.bfloat16, jnp.int32
MESH = pl.DeviceIdType.MESH
EDGE = 8
STEP = 20
UC = 32
RS_ROWS = 48


def dot(a, b):
    return jnp.dot(a, b, preferred_element_type=F32)


def dot_nt(a, b):
    return lax.dot_general(a, b, (((1,), (1,)), ((), ())), preferred_element_type=F32)


def split(x):
    hi = x.astype(BF16)
    return hi, (x - hi.astype(F32)).astype(BF16)


def iota(shape, axis):
    return lax.broadcasted_iota(I32, shape, axis)


def ones_where(mask):
    return jnp.where(mask, 1.0, 0.0).astype(F32)


def band(taps, first, offset, rows, phi_lane):
    along = jnp.concatenate([taps, jnp.zeros((112, 128), F32)], axis=0).T
    t_out = iota((128, 128), 0) & 15
    shift = t_out - (iota((128, 128), 1) + offset) + EDGE
    mixed = jnp.zeros((128, 128), F32)
    for s in range(2 * EDGE + 1):
        mixed = mixed + jnp.where(shift == s, along[s : s + 1, :], 0.0)
    wide = 32 * rows
    lane = iota((128, wide), 1)
    spread = ones_where(iota((128, wide), 0) == ((lane >> 4) & (rows - 1)) + first).astype(BF16)
    row = iota((128, wide), 0)
    same = (row >> 6) == (lane // (16 * rows))
    keep = ones_where(same & ((lane & 15) == phi_lane + ((row >> 4) & 3)))
    hi, lo = split(mixed)
    return (dot(hi, spread) * keep).astype(BF16), (dot(lo, spread) * keep).astype(BF16)


def kernel(
    lon,
    colat,
    pattern_hbm,
    phi_filter_hbm,
    partners_hbm,
    ops_hbm,
    taps_hbm,
    returns_hbm,
    count,
    table,
    weight,
    out,
    pattern,
    phi_filter,
    partners,
    ops,
    taps,
    returns,
    outbox,
    inbox,
    ybuf,
    tab,
    tcat_hi,
    tcat_lo,
    tab_t,
    src,
    place,
    fold,
    wide_ops,
    wide_partners,
    rcat,
    factors,
    picks,
    lw_own,
    lw_prev,
    lw_next,
    tapsbox,
    acc,
    rs_out,
    rs_in,
    gbd_hi,
    gbd_lo,
    ohret,
    outbox2,
    inbox2,
    load_sem,
    local_sem,
    halo_send,
    halo_recv,
    a_send,
    a_recv,
    rs_send,
    rs_recv,
    b_send,
    b_recv,
):
    i = lax.axis_index("lon")
    k = lax.axis_index("colat")
    prev_k = lax.rem(k + colat - 1, colat)
    next_k = lax.rem(k + 1, colat)
    nops8 = table.shape[0]
    theta = table.shape[1]
    npart = partners.shape[0]

    barrier = pltpu.get_barrier_semaphore()

    def peer(n):
        step = ((n + 1) // 2) * (1 - 2 * (n & 1))
        return lax.rem(i + lon // 2 + step, lon)

    def greet_lon(n, carry):
        pl.semaphore_signal(barrier, inc=1, device_id={"lon": peer(n)}, device_id_type=MESH)
        return carry

    def greet_colat(s, carry):
        pl.semaphore_signal(barrier, inc=1, device_id={"colat": lax.rem(k + s, colat)}, device_id_type=MESH)
        return carry

    lax.fori_loop(0, lon - 1, greet_lon, 0)
    lax.fori_loop(1, colat, greet_colat, 0)

    block = pl.multiple_of(lax.div(i, 4) * 16, 16)
    loads = [
        pltpu.make_async_copy(a, b, load_sem.at[n])
        for n, (a, b) in enumerate(
            (
                (phi_filter_hbm, phi_filter),
                (pattern_hbm, pattern),
                (taps_hbm, taps),
                (ops_hbm, ops),
                (partners_hbm, partners),
                (returns_hbm, returns),
            )
        )
    ]
    for load in loads:
        load.start()
    load_table = pltpu.make_async_copy(table, tab.at[pl.ds(0, nops8)], local_sem.at[0])
    load_table.start()
    load_lw = pltpu.make_async_copy(weight.at[:, :, pl.ds(block, 16), :], lw_own, local_sem.at[1])
    load_lw.start()

    for load in loads:
        load.wait()

    rows2 = jnp.concatenate([pattern[...], pattern[...]], axis=0)
    filtered = dot(rows2, phi_filter[...]).astype(BF16).astype(F32)
    ybuf[...] = filtered.T
    left = iota((lon, 128), 1) < 64
    for h in range(2):
        low = ybuf[pl.ds(2 * h, lon, stride=4), :]
        high = ybuf[pl.ds(2 * h + 1, lon, stride=4), :]
        outbox[:, h, :] = jnp.where(left, low, high)
    tapsbox[0, :, 0:17] = taps[...]

    pl.semaphore_wait(barrier, lon + colat - 2)

    def send_a(n, carry):
        to = peer(n)
        pltpu.make_async_remote_copy(
            src_ref=outbox.at[to],
            dst_ref=inbox.at[i],
            send_sem=a_send,
            recv_sem=a_recv,
            device_id={"lon": to},
            device_id_type=MESH,
        ).start()
        return carry

    lax.fori_loop(0, lon - 1, send_a, 0)
    keep_a = pltpu.make_async_copy(outbox.at[i], inbox.at[i], local_sem.at[2])
    keep_a.start()

    halos = []
    for n, (part, first, dst, to) in enumerate(((lw_prev, 8, 1, next_k), (lw_next, 0, 2, prev_k))):
        halos.append(
            pltpu.make_async_remote_copy(
                src_ref=weight.at[:, pl.ds(first, 8), pl.ds(block, 16), :],
                dst_ref=part,
                send_sem=halo_send.at[2 * n],
                recv_sem=halo_recv.at[2 * n],
                device_id={"colat": to},
                device_id_type=MESH,
            )
        )
        halos.append(
            pltpu.make_async_remote_copy(
                src_ref=tapsbox.at[0],
                dst_ref=tapsbox.at[dst],
                send_sem=halo_send.at[2 * n + 1],
                recv_sem=halo_recv.at[2 * n + 1],
                device_id={"colat": to},
                device_id_type=MESH,
            )
        )
    for copy in halos:
        copy.start()

    tab[pl.ds(nops8, tab.shape[0] - nops8), :] = jnp.zeros((tab.shape[0] - nops8, theta), F32)
    load_table.wait()
    ops_pad = tab.shape[0] // 8
    for part in range(8):
        hi, lo = split(tab[pl.ds(part, ops_pad, stride=8), :])
        tcat_hi[:, part * theta : (part + 1) * theta] = hi
        tcat_lo[:, part * theta : (part + 1) * theta] = lo
    n = iota((128, 8 * theta), 0)
    x = iota((128, 8 * theta), 1)
    match = ((x & (theta - 1)) == 16 * k + (n & 15)) & (x // theta == n >> 4)
    choose = ones_where(match).astype(BF16)
    tab_t[:, :ops_pad] = dot_nt(choose, tcat_hi[...]).astype(BF16)
    tab_t[:, ops_pad:] = dot_nt(choose, tcat_lo[...]).astype(BF16)
    for ref, index in ((wide_ops, ops), (wide_partners, partners)):
        index = index[...]
        ref[...] = jnp.concatenate([index, index[:, 128:]], axis=1)

    rows = [iota((r, 16, 256), 0) * 16 + iota((r, 16, 256), 1) for r in (16, ops_pad // 16 - 16)]
    rows = [r.astype(F32).astype(BF16) for r in rows]

    def hot(index, rows):
        index = jnp.broadcast_to(index, (16, 256)).astype(F32).astype(BF16)
        mask = rows == index[None]
        return jnp.where(mask, jnp.ones((), BF16), jnp.zeros((), BF16)).reshape(-1, 256)

    def gather_factors(p, carry):
        op = wide_ops[pl.ds(p, 1), :]
        first, second = hot(op, rows[0]), hot(op - 256, rows[1])
        factors[p] = dot(tab_t[...], jnp.concatenate([first, second, first, second], axis=0))
        partner = wide_partners[pl.ds(p, 1), :]
        picks[p] = hot((partner & 1) * 128 + (partner >> 1), rows[0])
        return carry

    lax.fori_loop(0, npart, gather_factors, 0, unroll=2)

    load_lw.wait()
    for copy in halos:
        copy.wait_recv()
    phi_lane = 4 * lax.rem(i, 4)
    users = weight.shape[3]
    folded = jnp.zeros((128, users), F32)
    for part, (box, first, offset, rows) in enumerate(
        ((lw_own, 0, 0, 16), (lw_prev, 8, -16, 8), (lw_next, 0, 16, 8))
    ):
        hi, lo = band(tapsbox[part], first, offset, rows, phi_lane)
        leaf = box[...].reshape(32 * rows, users)
        term = dot(hi, leaf) + dot(lo, leaf)
        if part == 1:
            term = jnp.where(k > 0, term, 0.0)
        if part == 2:
            term = jnp.where(k < colat - 1, term, 0.0)
        folded = folded + term
    fold_hi, fold_lo = split(folded.T)
    fold[...] = jnp.concatenate([fold_hi, fold_hi, fold_lo], axis=1)

    gbd_hi[...] = jnp.zeros(gbd_hi.shape, BF16)
    gbd_lo[...] = jnp.zeros(gbd_lo.shape, BF16)
    rcat[...] = jnp.zeros(rcat.shape, BF16)
    slots = returns.shape[0]
    listed = jnp.concatenate([returns[...], jnp.zeros((slots, 128 - lon), I32)], axis=1)
    listed = jnp.concatenate([listed, jnp.zeros((128 - slots, 128), I32)], axis=0).astype(F32).T
    for r in range(slots):
        column = listed[:lon, r : r + 1].astype(I32)
        ohret[:, r * 256 : (r + 1) * 256] = ones_where(iota((lon, 256), 1) == column).astype(BF16)

    xn = iota((256, 256), 0)
    xk = iota((256, 256), 1)
    phi = ((xk >> 7) & 1) * 2 + ((xk >> 6) & 1)
    match = (
        ((xk & 15) == (xn & 15))
        & (phi == ((xn >> 4) & 3))
        & (((xk >> 4) & 1) == ((xn >> 6) & 1))
        & (((xk >> 5) & 1) == (xn >> 7))
    )
    place[...] = ones_where(match).astype(BF16)
    keep_a.wait()
    pltpu.make_async_copy(inbox.at[pl.ds(0, lon - 1)], inbox.at[pl.ds(0, lon - 1)], a_recv).wait()
    rcat[:lon, :] = jnp.concatenate([inbox[:, 0, :], inbox[:, 1, :]], axis=1).astype(BF16)
    columns = dot_nt(place[...], rcat[...]).astype(BF16)
    src[:, :128] = columns[:128]
    src[:, 128:] = columns[128:]

    acc[...] = jnp.zeros(acc.shape, F32)

    def translate(g, carry):
        real = jnp.zeros((64, 256), F32)
        imag = jnp.zeros((64, 256), F32)
        for q in range(STEP):
            s = dot(src[...], picks[STEP * g + q])
            f = factors[STEP * g + q]
            real = real + (f[:64] * s[:64] - f[64:] * s[64:])
            imag = imag + (f[:64] * s[64:] + f[64:] * s[:64])
        acc[:64, :] += real
        acc[64:, :] += imag
        return carry

    lax.fori_loop(0, npart // STEP, translate, 0)
    t_hi, t_lo = split(acc[...])
    partial = dot(fold[...], jnp.concatenate([t_hi, t_lo, t_hi], axis=0))

    for c in range(colat):
        mine = partial[c * UC : (c + 1) * UC, :]
        tail = jnp.where(iota((16, 128), 1) < 64, mine[:16, 128:], mine[16:, 128:])
        rs_out[c] = jnp.concatenate([mine[:, :128], tail], axis=0).astype(BF16)

    def send_rs(s, carry):
        to = lax.rem(k + s, colat)
        pltpu.make_async_remote_copy(
            src_ref=rs_out.at[to],
            dst_ref=rs_in.at[k],
            send_sem=rs_send,
            recv_sem=rs_recv,
            device_id={"colat": to},
            device_id_type=MESH,
        ).start()
        return carry

    lax.fori_loop(1, colat, send_rs, 0)
    keep_rs = pltpu.make_async_copy(rs_out.at[k], rs_in.at[k], local_sem.at[3])
    keep_rs.start()
    keep_rs.wait()
    pltpu.make_async_copy(rs_in.at[pl.ds(0, colat - 1)], rs_in.at[pl.ds(0, colat - 1)], rs_recv).wait()
    total = rs_in[0].astype(F32)
    for c in range(1, colat):
        total = total + rs_in[c].astype(F32)
    tail = jnp.concatenate([total[UC:, :], pltpu.roll(total[UC:, :], 64, 1)], axis=0)
    tail = jnp.where(iota((UC, 128), 1) < 64, tail, 0.0)
    g_hi, g_lo = split(jnp.concatenate([total[:UC, :], tail], axis=1))
    for r in range(4):
        gbd_hi[r * UC : (r + 1) * UC, r * 256 : (r + 1) * 256] = g_hi
        gbd_lo[r * UC : (r + 1) * UC, r * 256 : (r + 1) * 256] = g_lo
    outbox2[:, 0, :] = dot_nt(ohret[:, :1024], gbd_hi[...]) + dot_nt(ohret[:, :1024], gbd_lo[...])
    outbox2[:, 1, :] = dot_nt(ohret[:, 1024:], gbd_hi[:, :256]) + dot_nt(ohret[:, 1024:], gbd_lo[:, :256])

    def send_b(n, carry):
        to = peer(n)
        pltpu.make_async_remote_copy(
            src_ref=outbox2.at[to],
            dst_ref=inbox2.at[i],
            send_sem=b_send,
            recv_sem=b_recv,
            device_id={"lon": to},
            device_id_type=MESH,
        ).start()
        return carry

    lax.fori_loop(0, lon - 1, send_b, 0)
    keep_b = pltpu.make_async_copy(outbox2.at[i], inbox2.at[i], local_sem.at[4])
    keep_b.start()
    keep_b.wait()
    pltpu.make_async_copy(inbox2.at[pl.ds(0, lon - 1)], inbox2.at[pl.ds(0, lon - 1)], b_recv).wait()
    field = jnp.sum(inbox2[...], axis=0)
    result = jnp.concatenate([field[0:1, r * UC : (r + 1) * UC] for r in range(4)] + [field[1:2, :UC]], axis=0)
    out[0] = jnp.where(iota((slots, UC), 0) < count[0], result, 0.0)

    for copy in halos:
        copy.wait_send()
    pltpu.make_async_copy(outbox.at[pl.ds(0, lon - 1)], outbox.at[pl.ds(0, lon - 1)], a_send).wait()
    pltpu.make_async_copy(rs_out.at[pl.ds(0, colat - 1)], rs_out.at[pl.ds(0, colat - 1)], rs_send).wait()
    pltpu.make_async_copy(outbox2.at[pl.ds(0, lon - 1)], outbox2.at[pl.ds(0, lon - 1)], b_send).wait()


def body(
    lon,
    colat,
    pattern,
    phi_filter,
    trans_table,
    partners,
    op_index,
    anter_weight,
    return_boxes,
    return_count,
    leaf_weight,
):
    nops, _, theta, _ = trans_table.shape
    npart, nbox = partners.shape[1], partners.shape[0]
    slots = return_boxes.shape[1]
    phi = phi_filter.shape[0]
    users = leaf_weight.shape[3]
    ops_pad = -(-nops // 128) * 128
    vmem, hbm = pl.BlockSpec(memory_space=pltpu.VMEM), pl.BlockSpec(memory_space=pl.ANY)
    smem = pl.BlockSpec(memory_space=pltpu.SMEM)
    return pl.pallas_call(
        functools.partial(kernel, lon, colat),
        out_shape=jax.ShapeDtypeStruct((1, slots, users // colat), F32),
        in_specs=[hbm, hbm, hbm, hbm, hbm, hbm, smem, hbm, hbm],
        out_specs=vmem,
        scratch_shapes=[
            pltpu.VMEM((pattern.size // phi, phi), BF16),
            pltpu.VMEM((phi, phi), BF16),
            pltpu.VMEM((npart, nbox), I32),
            pltpu.VMEM((npart, nbox), I32),
            pltpu.VMEM(anter_weight.shape[::-1], F32),
            pltpu.VMEM(return_boxes.shape[::-1], I32),
            pltpu.VMEM((lon, 2, 128), F32),
            pltpu.VMEM((lon, 2, 128), F32),
            pltpu.VMEM((phi, 128), F32),
            pltpu.VMEM((ops_pad * 8, theta), F32),
            pltpu.VMEM((ops_pad, 8 * theta), BF16),
            pltpu.VMEM((ops_pad, 8 * theta), BF16),
            pltpu.VMEM((128, 2 * ops_pad), BF16),
            pltpu.VMEM((128, 256), BF16),
            pltpu.VMEM((256, 256), BF16),
            pltpu.VMEM((users, 384), BF16),
            pltpu.VMEM((npart, 256), I32),
            pltpu.VMEM((npart, 256), I32),
            pltpu.VMEM((128, 256), BF16),
            pltpu.VMEM((npart, 128, 256), F32),
            pltpu.VMEM((npart, 256, 256), BF16),
            pltpu.VMEM((2, 16, 16, users), BF16),
            pltpu.VMEM((2, 8, 16, users), BF16),
            pltpu.VMEM((2, 8, 16, users), BF16),
            pltpu.VMEM((3, 16, 128), F32),
            pltpu.VMEM((128, 256), F32),
            pltpu.VMEM((colat, RS_ROWS, 128), BF16),
            pltpu.VMEM((colat, RS_ROWS, 128), BF16),
            pltpu.VMEM((128, 1024), BF16),
            pltpu.VMEM((128, 1024), BF16),
            pltpu.VMEM((lon, slots * 256), BF16),
            pltpu.VMEM((lon, 2, 128), F32),
            pltpu.VMEM((lon, 2, 128), F32),
            pltpu.SemaphoreType.DMA((6,)),
            pltpu.SemaphoreType.DMA((5,)),
            pltpu.SemaphoreType.DMA((4,)),
            pltpu.SemaphoreType.DMA((4,)),
            pltpu.SemaphoreType.DMA,
            pltpu.SemaphoreType.DMA,
            pltpu.SemaphoreType.DMA,
            pltpu.SemaphoreType.DMA,
            pltpu.SemaphoreType.DMA,
            pltpu.SemaphoreType.DMA,
        ],
        compiler_params=pltpu.CompilerParams(
            collective_id=0, has_side_effects=True, vmem_limit_bytes=60 * 1024 * 1024
        ),
        name="mlfma_pass",
    )(
        pattern.reshape(-1, phi),
        phi_filter,
        partners.T,
        op_index.T,
        anter_weight.T,
        return_boxes.T,
        return_count,
        trans_table.transpose(0, 1, 3, 2).reshape(nops * 8, theta),
        leaf_weight,
    )


def solution(mesh):
    in_specs = (
        P("lon", None, "colat", None),
        P(),
        P(None, None, None, "lon"),
        P(),
        P(),
        P(None, "colat"),
        P(),
        P("lon"),
        P(None, "colat", None, None),
    )
    out_specs = P("lon", None, "colat")
    run = functools.partial(body, mesh.shape["lon"], mesh.shape["colat"])
    return jax.shard_map(run, mesh=mesh, in_specs=in_specs, out_specs=out_specs, check_vma=False)
```

```python
import functools

import jax
import jax.numpy as jnp
from jax import lax
from jax.experimental import pallas as pl
from jax.experimental.pallas import tpu as pltpu
from jax.sharding import PartitionSpec as P

F32, BF16, I32 = jnp.float32, jnp.bfloat16, jnp.int32
MESH = pl.DeviceIdType.MESH
EDGE = 8
X = 4
STEP = 40
UC = 32
RS_ROWS = 48


def dot(a, b):
    return jnp.dot(a, b, preferred_element_type=F32)


def dot_nt(a, b):
    return lax.dot_general(a, b, (((1,), (1,)), ((), ())), preferred_element_type=F32)


def split(x):
    hi = x.astype(BF16)
    return hi, (x - hi.astype(F32)).astype(BF16)


def iota(shape, axis):
    return lax.broadcasted_iota(I32, shape, axis)


def ones_where(mask):
    return jnp.where(mask, 1.0, 0.0).astype(F32)


def band(taps, first, offset, rows, phi_lane):
    along = jnp.concatenate([taps, jnp.zeros((112, 128), F32)], axis=0).T
    t_out = iota((128, 128), 0) & 15
    shift = t_out - (iota((128, 128), 1) + offset) + EDGE
    mixed = jnp.zeros((128, 128), F32)
    for s in range(2 * EDGE + 1):
        mixed = mixed + jnp.where(shift == s, along[s : s + 1, :], 0.0)
    wide = 32 * rows
    lane = iota((128, wide), 1)
    spread = ones_where(iota((128, wide), 0) == ((lane >> 4) & (rows - 1)) + first).astype(BF16)
    row = iota((128, wide), 0)
    same = (row >> 6) == (lane // (16 * rows))
    keep = ones_where(same & ((lane & 15) == phi_lane + ((row >> 4) & 3)))
    hi, lo = split(mixed)
    return (dot(hi, spread) * keep).astype(BF16), (dot(lo, spread) * keep).astype(BF16)


def kernel(
    lon,
    colat,
    pattern_hbm,
    phi_filter_hbm,
    partners_hbm,
    ops_hbm,
    taps_hbm,
    returns_hbm,
    count,
    table,
    weight,
    out,
    pattern,
    phi_filter,
    partners,
    ops,
    taps,
    returns,
    outbox,
    inbox,
    ybuf,
    tab,
    tcat_hi,
    tcat_lo,
    tab_t,
    src,
    place,
    fold,
    wide_ops,
    wide_partners,
    rcat,
    factors,
    picks,
    lw_own,
    lw_prev,
    lw_next,
    tapsbox,
    acc,
    rs_out,
    rs_in,
    gbd_hi,
    gbd_lo,
    ohret,
    outbox2,
    inbox2,
    load_sem,
    local_sem,
    halo_send,
    halo_recv,
    a_send,
    a_recv,
    rs_send,
    rs_recv,
    b_send,
    b_recv,
):
    i = lax.axis_index("lon")
    k = lax.axis_index("colat")
    prev_k = lax.rem(k + colat - 1, colat)
    next_k = lax.rem(k + 1, colat)
    nops8 = table.shape[0]
    theta = table.shape[1]
    npart = partners.shape[0]

    barrier = pltpu.get_barrier_semaphore()

    z_size = lon // (2 * X)
    here_z, here_y, here_x = lax.div(i, 2 * X), lax.rem(lax.div(i, X), 2), lax.rem(i, X)
    along_x = [lax.rem(here_x + offset, X) for offset in (2, 1, 3, 0)]

    def for_peers(act):
        for row, rings in (((1 - here_y) * X, z_size), (here_y * X, z_size - 1)):

            def ring(a, carry):
                step = ((a + 1) >> 1) * (1 - 2 * (a & 1))
                z = lax.rem(here_z + z_size // 2 + step, z_size)
                for x in along_x:
                    act(z * (2 * X) + row + x)
                return carry

            lax.fori_loop(0, rings, ring, 0)
        for x in along_x[:3]:
            act(here_z * (2 * X) + here_y * X + x)

    def greet(to):
        pl.semaphore_signal(barrier, inc=1, device_id={"lon": to}, device_id_type=MESH)

    def greet_colat(s, carry):
        pl.semaphore_signal(barrier, inc=1, device_id={"colat": lax.rem(k + s, colat)}, device_id_type=MESH)
        return carry

    for_peers(greet)
    lax.fori_loop(1, colat, greet_colat, 0)

    block = pl.multiple_of(lax.div(i, 4) * 16, 16)
    loads = [
        pltpu.make_async_copy(a, b, load_sem.at[n])
        for n, (a, b) in enumerate(
            (
                (phi_filter_hbm, phi_filter),
                (pattern_hbm, pattern),
                (taps_hbm, taps),
                (ops_hbm, ops),
                (partners_hbm, partners),
                (returns_hbm, returns),
            )
        )
    ]
    for load in loads:
        load.start()
    load_table = pltpu.make_async_copy(table, tab.at[pl.ds(0, nops8)], local_sem.at[0])
    load_table.start()
    load_lw = pltpu.make_async_copy(weight.at[:, :, pl.ds(block, 16), :], lw_own, local_sem.at[1])
    load_lw.start()

    for load in loads:
        load.wait()

    rows2 = jnp.concatenate([pattern[...], pattern[...]], axis=0)
    filtered = dot(rows2, phi_filter[...]).astype(BF16).astype(F32)
    ybuf[...] = filtered.T
    left = iota((lon, 128), 1) < 64
    for h in range(2):
        low = ybuf[pl.ds(2 * h, lon, stride=4), :]
        high = ybuf[pl.ds(2 * h + 1, lon, stride=4), :]
        outbox[:, h, :] = jnp.where(left, low, high)
    tapsbox[0, :, 0:17] = taps[...]

    pl.semaphore_wait(barrier, lon + colat - 2)

    def send_a(to):
        pltpu.make_async_remote_copy(
            src_ref=outbox.at[to],
            dst_ref=inbox.at[i],
            send_sem=a_send,
            recv_sem=a_recv,
            device_id={"lon": to},
            device_id_type=MESH,
        ).start()

    for_peers(send_a)
    keep_a = pltpu.make_async_copy(outbox.at[i], inbox.at[i], local_sem.at[2])
    keep_a.start()

    halos = []
    for n, (part, first, dst, to) in enumerate(((lw_prev, 8, 1, next_k), (lw_next, 0, 2, prev_k))):
        halos.append(
            pltpu.make_async_remote_copy(
                src_ref=weight.at[:, pl.ds(first, 8), pl.ds(block, 16), :],
                dst_ref=part,
                send_sem=halo_send.at[2 * n],
                recv_sem=halo_recv.at[2 * n],
                device_id={"colat": to},
                device_id_type=MESH,
            )
        )
        halos.append(
            pltpu.make_async_remote_copy(
                src_ref=tapsbox.at[0],
                dst_ref=tapsbox.at[dst],
                send_sem=halo_send.at[2 * n + 1],
                recv_sem=halo_recv.at[2 * n + 1],
                device_id={"colat": to},
                device_id_type=MESH,
            )
        )
    for copy in halos:
        copy.start()

    tab[pl.ds(nops8, tab.shape[0] - nops8), :] = jnp.zeros((tab.shape[0] - nops8, theta), F32)
    load_table.wait()
    ops_pad = tab.shape[0] // 8
    for part in range(8):
        hi, lo = split(tab[pl.ds(part, ops_pad, stride=8), :])
        tcat_hi[:, part * theta : (part + 1) * theta] = hi
        tcat_lo[:, part * theta : (part + 1) * theta] = lo
    n = iota((128, 8 * theta), 0)
    x = iota((128, 8 * theta), 1)
    match = ((x & (theta - 1)) == 16 * k + (n & 15)) & (x // theta == n >> 4)
    choose = ones_where(match).astype(BF16)
    tab_t[:, :ops_pad] = dot_nt(choose, tcat_hi[...]).astype(BF16)
    tab_t[:, ops_pad:] = dot_nt(choose, tcat_lo[...]).astype(BF16)
    for ref, index in ((wide_ops, ops), (wide_partners, partners)):
        index = index[...]
        ref[...] = jnp.concatenate([index, index[:, 128:]], axis=1)

    rows = [iota((r, 16, 256), 0) * 16 + iota((r, 16, 256), 1) for r in (16, ops_pad // 16 - 16)]
    rows = [r.astype(F32).astype(BF16) for r in rows]

    def hot(index, rows):
        index = jnp.broadcast_to(index, (16, 256)).astype(F32).astype(BF16)
        mask = rows == index[None]
        return jnp.where(mask, jnp.ones((), BF16), jnp.zeros((), BF16)).reshape(-1, 256)

    def gather_factors(p, carry):
        op = wide_ops[pl.ds(p, 1), :]
        first, second = hot(op, rows[0]), hot(op - 256, rows[1])
        factors[p] = dot(tab_t[...], jnp.concatenate([first, second, first, second], axis=0))
        partner = wide_partners[pl.ds(p, 1), :]
        picks[p] = hot((partner & 1) * 128 + (partner >> 1), rows[0])
        return carry

    lax.fori_loop(0, npart, gather_factors, 0, unroll=2)

    load_lw.wait()
    for copy in halos:
        copy.wait_recv()
    phi_lane = 4 * lax.rem(i, 4)
    users = weight.shape[3]
    folded = jnp.zeros((128, users), F32)
    for part, (box, first, offset, rows) in enumerate(
        ((lw_own, 0, 0, 16), (lw_prev, 8, -16, 8), (lw_next, 0, 16, 8))
    ):
        hi, lo = band(tapsbox[part], first, offset, rows, phi_lane)
        leaf = box[...].reshape(32 * rows, users)
        term = dot(hi, leaf) + dot(lo, leaf)
        if part == 1:
            term = jnp.where(k > 0, term, 0.0)
        if part == 2:
            term = jnp.where(k < colat - 1, term, 0.0)
        folded = folded + term
    fold_hi, fold_lo = split(folded.T)
    fold[...] = jnp.concatenate([fold_hi, fold_hi, fold_lo], axis=1)

    gbd_hi[...] = jnp.zeros(gbd_hi.shape, BF16)
    gbd_lo[...] = jnp.zeros(gbd_lo.shape, BF16)
    rcat[...] = jnp.zeros(rcat.shape, BF16)
    slots = returns.shape[0]
    listed = jnp.concatenate([returns[...], jnp.zeros((slots, 128 - lon), I32)], axis=1)
    listed = jnp.concatenate([listed, jnp.zeros((128 - slots, 128), I32)], axis=0).astype(F32).T
    for r in range(slots):
        column = listed[:lon, r : r + 1].astype(I32)
        ohret[:, r * 256 : (r + 1) * 256] = ones_where(iota((lon, 256), 1) == column).astype(BF16)

    xn = iota((256, 256), 0)
    xk = iota((256, 256), 1)
    phi = ((xk >> 7) & 1) * 2 + ((xk >> 6) & 1)
    match = (
        ((xk & 15) == (xn & 15))
        & (phi == ((xn >> 4) & 3))
        & (((xk >> 4) & 1) == ((xn >> 6) & 1))
        & (((xk >> 5) & 1) == (xn >> 7))
    )
    place[...] = ones_where(match).astype(BF16)
    keep_a.wait()
    pltpu.make_async_copy(inbox.at[pl.ds(0, lon - 1)], inbox.at[pl.ds(0, lon - 1)], a_recv).wait()
    rcat[:lon, :] = jnp.concatenate([inbox[:, 0, :], inbox[:, 1, :]], axis=1).astype(BF16)
    columns = dot_nt(place[...], rcat[...]).astype(BF16)
    src[:, :128] = columns[:128]
    src[:, 128:] = columns[128:]

    acc[...] = jnp.zeros(acc.shape, F32)

    def translate(g, carry):
        real = jnp.zeros((64, 256), F32)
        imag = jnp.zeros((64, 256), F32)
        for q in range(STEP):
            s = dot(src[...], picks[STEP * g + q])
            f = factors[STEP * g + q]
            real = real + (f[:64] * s[:64] - f[64:] * s[64:])
            imag = imag + (f[:64] * s[64:] + f[64:] * s[:64])
        acc[:64, :] += real
        acc[64:, :] += imag
        return carry

    lax.fori_loop(0, npart // STEP, translate, 0)
    t_hi, t_lo = split(acc[...])
    partial = dot(fold[...], jnp.concatenate([t_hi, t_lo, t_hi], axis=0))

    for c in range(colat):
        mine = partial[c * UC : (c + 1) * UC, :]
        tail = jnp.where(iota((16, 128), 1) < 64, mine[:16, 128:], mine[16:, 128:])
        rs_out[c] = jnp.concatenate([mine[:, :128], tail], axis=0).astype(BF16)

    def send_rs(s, carry):
        to = lax.rem(k + s, colat)
        pltpu.make_async_remote_copy(
            src_ref=rs_out.at[to],
            dst_ref=rs_in.at[k],
            send_sem=rs_send,
            recv_sem=rs_recv,
            device_id={"colat": to},
            device_id_type=MESH,
        ).start()
        return carry

    lax.fori_loop(1, colat, send_rs, 0)
    keep_rs = pltpu.make_async_copy(rs_out.at[k], rs_in.at[k], local_sem.at[3])
    keep_rs.start()
    keep_rs.wait()
    pltpu.make_async_copy(rs_in.at[pl.ds(0, colat - 1)], rs_in.at[pl.ds(0, colat - 1)], rs_recv).wait()
    total = rs_in[0].astype(F32)
    for c in range(1, colat):
        total = total + rs_in[c].astype(F32)
    tail = jnp.concatenate([total[UC:, :], pltpu.roll(total[UC:, :], 64, 1)], axis=0)
    tail = jnp.where(iota((UC, 128), 1) < 64, tail, 0.0)
    g_hi, g_lo = split(jnp.concatenate([total[:UC, :], tail], axis=1))
    for r in range(4):
        gbd_hi[r * UC : (r + 1) * UC, r * 256 : (r + 1) * 256] = g_hi
        gbd_lo[r * UC : (r + 1) * UC, r * 256 : (r + 1) * 256] = g_lo
    outbox2[:, 0, :] = dot_nt(ohret[:, :1024], gbd_hi[...]) + dot_nt(ohret[:, :1024], gbd_lo[...])
    outbox2[:, 1, :] = dot_nt(ohret[:, 1024:], gbd_hi[:, :256]) + dot_nt(ohret[:, 1024:], gbd_lo[:, :256])

    def send_b(to):
        pltpu.make_async_remote_copy(
            src_ref=outbox2.at[to],
            dst_ref=inbox2.at[i],
            send_sem=b_send,
            recv_sem=b_recv,
            device_id={"lon": to},
            device_id_type=MESH,
        ).start()

    for_peers(send_b)
    keep_b = pltpu.make_async_copy(outbox2.at[i], inbox2.at[i], local_sem.at[4])
    keep_b.start()
    keep_b.wait()
    pltpu.make_async_copy(inbox2.at[pl.ds(0, lon - 1)], inbox2.at[pl.ds(0, lon - 1)], b_recv).wait()
    field = jnp.sum(inbox2[...], axis=0)
    result = jnp.concatenate([field[0:1, r * UC : (r + 1) * UC] for r in range(4)] + [field[1:2, :UC]], axis=0)
    out[:, 0, :] = jnp.where(iota((slots, UC), 0) < count[0], result, 0.0)

    for copy in halos:
        copy.wait_send()
    pltpu.make_async_copy(outbox.at[pl.ds(0, lon - 1)], outbox.at[pl.ds(0, lon - 1)], a_send).wait()
    pltpu.make_async_copy(rs_out.at[pl.ds(0, colat - 1)], rs_out.at[pl.ds(0, colat - 1)], rs_send).wait()
    pltpu.make_async_copy(outbox2.at[pl.ds(0, lon - 1)], outbox2.at[pl.ds(0, lon - 1)], b_send).wait()


def body(
    lon,
    colat,
    pattern,
    phi_filter,
    trans_table,
    partners,
    op_index,
    anter_weight,
    return_boxes,
    return_count,
    leaf_weight,
):
    nops, _, theta, _ = trans_table.shape
    npart, nbox = partners.shape[1], partners.shape[0]
    slots = return_boxes.shape[1]
    phi = phi_filter.shape[0]
    users = leaf_weight.shape[3]
    ops_pad = -(-nops // 128) * 128
    vmem, hbm = pl.BlockSpec(memory_space=pltpu.VMEM), pl.BlockSpec(memory_space=pl.ANY)
    smem = pl.BlockSpec(memory_space=pltpu.SMEM)
    return pl.pallas_call(
        functools.partial(kernel, lon, colat),
        out_shape=jax.ShapeDtypeStruct((slots, 1, users // colat), F32),
        in_specs=[hbm, hbm, hbm, hbm, hbm, hbm, smem, hbm, hbm],
        out_specs=vmem,
        scratch_shapes=[
            pltpu.VMEM((pattern.size // phi, phi), BF16),
            pltpu.VMEM((phi, phi), BF16),
            pltpu.VMEM((npart, nbox), I32),
            pltpu.VMEM((npart, nbox), I32),
            pltpu.VMEM(anter_weight.shape[::-1], F32),
            pltpu.VMEM(return_boxes.shape[::-1], I32),
            pltpu.VMEM((lon, 2, 128), F32),
            pltpu.VMEM((lon, 2, 128), F32),
            pltpu.VMEM((phi, 128), F32),
            pltpu.VMEM((ops_pad * 8, theta), F32),
            pltpu.VMEM((ops_pad, 8 * theta), BF16),
            pltpu.VMEM((ops_pad, 8 * theta), BF16),
            pltpu.VMEM((128, 2 * ops_pad), BF16),
            pltpu.VMEM((128, 256), BF16),
            pltpu.VMEM((256, 256), BF16),
            pltpu.VMEM((users, 384), BF16),
            pltpu.VMEM((npart, 256), I32),
            pltpu.VMEM((npart, 256), I32),
            pltpu.VMEM((128, 256), BF16),
            pltpu.VMEM((npart, 128, 256), F32),
            pltpu.VMEM((npart, 256, 256), BF16),
            pltpu.VMEM((2, 16, 16, users), BF16),
            pltpu.VMEM((2, 8, 16, users), BF16),
            pltpu.VMEM((2, 8, 16, users), BF16),
            pltpu.VMEM((3, 16, 128), F32),
            pltpu.VMEM((128, 256), F32),
            pltpu.VMEM((colat, RS_ROWS, 128), BF16),
            pltpu.VMEM((colat, RS_ROWS, 128), BF16),
            pltpu.VMEM((128, 1024), BF16),
            pltpu.VMEM((128, 1024), BF16),
            pltpu.VMEM((lon, slots * 256), BF16),
            pltpu.VMEM((lon, 2, 128), F32),
            pltpu.VMEM((lon, 2, 128), F32),
            pltpu.SemaphoreType.DMA((6,)),
            pltpu.SemaphoreType.DMA((5,)),
            pltpu.SemaphoreType.DMA((4,)),
            pltpu.SemaphoreType.DMA((4,)),
            pltpu.SemaphoreType.DMA,
            pltpu.SemaphoreType.DMA,
            pltpu.SemaphoreType.DMA,
            pltpu.SemaphoreType.DMA,
            pltpu.SemaphoreType.DMA,
            pltpu.SemaphoreType.DMA,
        ],
        compiler_params=pltpu.CompilerParams(
            collective_id=0, has_side_effects=True, vmem_limit_bytes=60 * 1024 * 1024
        ),
        name="mlfma_pass",
    )(
        pattern.reshape(-1, phi),
        phi_filter,
        partners.T,
        op_index.T,
        anter_weight.T,
        return_boxes.T,
        return_count,
        trans_table.transpose(0, 1, 3, 2).reshape(nops * 8, theta),
        leaf_weight,
    ).transpose(1, 0, 2)


def solution(mesh):
    in_specs = (
        P("lon", None, "colat", None),
        P(),
        P(None, None, None, "lon"),
        P(),
        P(),
        P(None, "colat"),
        P(),
        P("lon"),
        P(None, "colat", None, None),
    )
    out_specs = P("lon", None, "colat")
    run = functools.partial(body, mesh.shape["lon"], mesh.shape["colat"])
    return jax.shard_map(run, mesh=mesh, in_specs=in_specs, out_specs=out_specs, check_vma=False)
```

```python
import functools

import jax
import jax.numpy as jnp
from jax import lax
from jax.experimental import pallas as pl
from jax.experimental.pallas import tpu as pltpu
from jax.sharding import PartitionSpec as P

F32, BF16, I32 = jnp.float32, jnp.bfloat16, jnp.int32
MESH = pl.DeviceIdType.MESH
EDGE = 8
X = 4
STEP = 40
UC = 32
RS_ROWS = 48


def dot(a, b):
    return jnp.dot(a, b, preferred_element_type=F32)


def dot_nt(a, b):
    return lax.dot_general(a, b, (((1,), (1,)), ((), ())), preferred_element_type=F32)


def split(x):
    hi = x.astype(BF16)
    return hi, (x - hi.astype(F32)).astype(BF16)


def iota(shape, axis):
    return lax.broadcasted_iota(I32, shape, axis)


def ones_where(mask):
    return jnp.where(mask, 1.0, 0.0).astype(F32)


def band(taps, first, offset, rows, phi_lane):
    along = jnp.concatenate([taps, jnp.zeros((112, 128), F32)], axis=0).T
    t_out = iota((128, 128), 0) & 15
    shift = t_out - (iota((128, 128), 1) + offset) + EDGE
    mixed = jnp.zeros((128, 128), F32)
    for s in range(2 * EDGE + 1):
        mixed = mixed + jnp.where(shift == s, along[s : s + 1, :], 0.0)
    wide = 32 * rows
    lane = iota((128, wide), 1)
    spread = ones_where(iota((128, wide), 0) == ((lane >> 4) & (rows - 1)) + first).astype(BF16)
    row = iota((128, wide), 0)
    same = (row >> 6) == (lane // (16 * rows))
    keep = ones_where(same & ((lane & 15) == phi_lane + ((row >> 4) & 3)))
    hi, lo = split(mixed)
    return (dot(hi, spread) * keep).astype(BF16), (dot(lo, spread) * keep).astype(BF16)


def kernel(
    lon,
    colat,
    pattern_hbm,
    phi_filter_hbm,
    partners_hbm,
    ops_hbm,
    taps_hbm,
    returns_hbm,
    count_hbm,
    table,
    weight,
    out,
    pattern,
    phi_filter,
    partners,
    ops,
    taps,
    returns,
    count,
    outbox,
    inbox,
    ybuf,
    tab,
    tcat_hi,
    tcat_lo,
    tab_t,
    src,
    place,
    fold,
    wide_ops,
    wide_partners,
    rcat,
    factors,
    picks,
    lw_own,
    lw_prev,
    lw_next,
    tapsbox,
    acc,
    rs_out,
    rs_in,
    gbd_hi,
    gbd_lo,
    ohret,
    outbox2,
    inbox2,
    load_sem,
    local_sem,
    halo_send,
    halo_recv,
    a_send,
    a_recv,
    rs_send,
    rs_recv,
    b_send,
    b_recv,
):
    i = lax.axis_index("lon")
    k = lax.axis_index("colat")
    prev_k = lax.rem(k + colat - 1, colat)
    next_k = lax.rem(k + 1, colat)
    nops8 = table.shape[0]
    theta = table.shape[1]
    npart = partners.shape[0]

    barrier = pltpu.get_barrier_semaphore()

    z_size = lon // (2 * X)
    here_z, here_y, here_x = lax.div(i, 2 * X), lax.rem(lax.div(i, X), 2), lax.rem(i, X)
    along_x = [lax.rem(here_x + offset, X) for offset in (2, 1, 3, 0)]

    def for_peers(act):
        for row, rings in (((1 - here_y) * X, z_size), (here_y * X, z_size - 1)):

            def ring(a, carry):
                step = ((a + 1) >> 1) * (1 - 2 * (a & 1))
                z = lax.rem(here_z + z_size // 2 + step, z_size)
                for x in along_x:
                    act(z * (2 * X) + row + x)
                return carry

            lax.fori_loop(0, rings, ring, 0)
        for x in along_x[:3]:
            act(here_z * (2 * X) + here_y * X + x)

    def greet(to):
        pl.semaphore_signal(barrier, inc=1, device_id={"lon": to}, device_id_type=MESH)

    def greet_colat(s, carry):
        pl.semaphore_signal(barrier, inc=1, device_id={"colat": lax.rem(k + s, colat)}, device_id_type=MESH)
        return carry

    for_peers(greet)
    lax.fori_loop(1, colat, greet_colat, 0)

    block = pl.multiple_of(lax.div(i, 4) * 16, 16)
    loads = [
        pltpu.make_async_copy(a, b, load_sem.at[n])
        for n, (a, b) in enumerate(
            (
                (phi_filter_hbm, phi_filter),
                (pattern_hbm, pattern),
                (taps_hbm, taps),
                (ops_hbm, ops),
                (partners_hbm, partners),
                (returns_hbm, returns),
                (count_hbm, count),
            )
        )
    ]
    for load in loads:
        load.start()
    load_table = pltpu.make_async_copy(table, tab.at[pl.ds(0, nops8)], local_sem.at[0])
    load_table.start()
    load_lw = pltpu.make_async_copy(weight.at[:, :, pl.ds(block, 16), :], lw_own, local_sem.at[1])
    load_lw.start()

    for load in loads:
        load.wait()

    rows2 = jnp.concatenate([pattern[...], pattern[...]], axis=0)
    filtered = dot(rows2, phi_filter[...]).astype(BF16).astype(F32)
    ybuf[...] = filtered.T
    left = iota((lon, 128), 1) < 64
    for h in range(2):
        low = ybuf[pl.ds(2 * h, lon, stride=4), :]
        high = ybuf[pl.ds(2 * h + 1, lon, stride=4), :]
        outbox[:, h, :] = jnp.where(left, low, high)
    tapsbox[0, :, 0:17] = taps[...]

    pl.semaphore_wait(barrier, lon + colat - 2)

    def send_a(to):
        pltpu.make_async_remote_copy(
            src_ref=outbox.at[to],
            dst_ref=inbox.at[i],
            send_sem=a_send,
            recv_sem=a_recv,
            device_id={"lon": to},
            device_id_type=MESH,
        ).start()

    for_peers(send_a)
    keep_a = pltpu.make_async_copy(outbox.at[i], inbox.at[i], local_sem.at[2])
    keep_a.start()

    halos = []
    for n, (part, first, dst, to) in enumerate(((lw_prev, 8, 1, next_k), (lw_next, 0, 2, prev_k))):
        halos.append(
            pltpu.make_async_remote_copy(
                src_ref=weight.at[:, pl.ds(first, 8), pl.ds(block, 16), :],
                dst_ref=part,
                send_sem=halo_send.at[2 * n],
                recv_sem=halo_recv.at[2 * n],
                device_id={"colat": to},
                device_id_type=MESH,
            )
        )
        halos.append(
            pltpu.make_async_remote_copy(
                src_ref=tapsbox.at[0],
                dst_ref=tapsbox.at[dst],
                send_sem=halo_send.at[2 * n + 1],
                recv_sem=halo_recv.at[2 * n + 1],
                device_id={"colat": to},
                device_id_type=MESH,
            )
        )
    for copy in halos:
        copy.start()

    tab[pl.ds(nops8, tab.shape[0] - nops8), :] = jnp.zeros((tab.shape[0] - nops8, theta), F32)
    load_table.wait()
    ops_pad = tab.shape[0] // 8
    for part in range(8):
        hi, lo = split(tab[pl.ds(part, ops_pad, stride=8), :])
        tcat_hi[:, part * theta : (part + 1) * theta] = hi
        tcat_lo[:, part * theta : (part + 1) * theta] = lo
    n = iota((128, 8 * theta), 0)
    x = iota((128, 8 * theta), 1)
    match = ((x & (theta - 1)) == 16 * k + (n & 15)) & (x // theta == n >> 4)
    choose = ones_where(match).astype(BF16)
    tab_t[:, :ops_pad] = dot_nt(choose, tcat_hi[...]).astype(BF16)
    tab_t[:, ops_pad:] = dot_nt(choose, tcat_lo[...]).astype(BF16)
    for ref, index in ((wide_ops, ops), (wide_partners, partners)):
        index = index[...]
        ref[...] = jnp.concatenate([index, index[:, 128:]], axis=1)

    rows = [iota((r, 16, 256), 0) * 16 + iota((r, 16, 256), 1) for r in (16, ops_pad // 16 - 16)]
    rows = [r.astype(F32).astype(BF16) for r in rows]

    def hot(index, rows):
        index = jnp.broadcast_to(index, (16, 256)).astype(F32).astype(BF16)
        mask = rows == index[None]
        return jnp.where(mask, jnp.ones((), BF16), jnp.zeros((), BF16)).reshape(-1, 256)

    def gather_factors(p, carry):
        op = wide_ops[pl.ds(p, 1), :]
        first, second = hot(op, rows[0]), hot(op - 256, rows[1])
        factors[p] = dot(tab_t[...], jnp.concatenate([first, second, first, second], axis=0))
        partner = wide_partners[pl.ds(p, 1), :]
        picks[p] = hot((partner & 1) * 128 + (partner >> 1), rows[0])
        return carry

    lax.fori_loop(0, npart, gather_factors, 0, unroll=2)

    load_lw.wait()
    for copy in halos:
        copy.wait_recv()
    phi_lane = 4 * lax.rem(i, 4)
    users = weight.shape[3]
    folded = jnp.zeros((128, users), F32)
    for part, (box, first, offset, rows) in enumerate(
        ((lw_own, 0, 0, 16), (lw_prev, 8, -16, 8), (lw_next, 0, 16, 8))
    ):
        hi, lo = band(tapsbox[part], first, offset, rows, phi_lane)
        leaf = box[...].reshape(32 * rows, users)
        term = dot(hi, leaf) + dot(lo, leaf)
        if part == 1:
            term = jnp.where(k > 0, term, 0.0)
        if part == 2:
            term = jnp.where(k < colat - 1, term, 0.0)
        folded = folded + term
    fold_hi, fold_lo = split(folded.T)
    fold[...] = jnp.concatenate([fold_hi, fold_hi, fold_lo], axis=1)

    gbd_hi[...] = jnp.zeros(gbd_hi.shape, BF16)
    gbd_lo[...] = jnp.zeros(gbd_lo.shape, BF16)
    rcat[...] = jnp.zeros(rcat.shape, BF16)
    slots = returns.shape[0]
    listed = jnp.concatenate([returns[...], jnp.zeros((slots, 128 - lon), I32)], axis=1)
    listed = jnp.concatenate([listed, jnp.zeros((128 - slots, 128), I32)], axis=0).astype(F32).T
    for r in range(slots):
        column = listed[:lon, r : r + 1].astype(I32)
        ohret[:, r * 256 : (r + 1) * 256] = ones_where(iota((lon, 256), 1) == column).astype(BF16)

    xn = iota((256, 256), 0)
    xk = iota((256, 256), 1)
    phi = ((xk >> 7) & 1) * 2 + ((xk >> 6) & 1)
    match = (
        ((xk & 15) == (xn & 15))
        & (phi == ((xn >> 4) & 3))
        & (((xk >> 4) & 1) == ((xn >> 6) & 1))
        & (((xk >> 5) & 1) == (xn >> 7))
    )
    place[...] = ones_where(match).astype(BF16)
    keep_a.wait()
    pltpu.make_async_copy(inbox.at[pl.ds(0, lon - 1)], inbox.at[pl.ds(0, lon - 1)], a_recv).wait()
    rcat[:lon, :] = jnp.concatenate([inbox[:, 0, :], inbox[:, 1, :]], axis=1).astype(BF16)
    columns = dot_nt(place[...], rcat[...]).astype(BF16)
    src[:, :128] = columns[:128]
    src[:, 128:] = columns[128:]

    acc[...] = jnp.zeros(acc.shape, F32)

    def translate(g, carry):
        real = jnp.zeros((64, 256), F32)
        imag = jnp.zeros((64, 256), F32)
        for q in range(STEP):
            s = dot(src[...], picks[STEP * g + q])
            f = factors[STEP * g + q]
            real = real + (f[:64] * s[:64] - f[64:] * s[64:])
            imag = imag + (f[:64] * s[64:] + f[64:] * s[:64])
        acc[:64, :] += real
        acc[64:, :] += imag
        return carry

    lax.fori_loop(0, npart // STEP, translate, 0)
    t_hi, t_lo = split(acc[...])
    partial = dot(fold[...], jnp.concatenate([t_hi, t_lo, t_hi], axis=0))

    for c in range(colat):
        mine = partial[c * UC : (c + 1) * UC, :]
        tail = jnp.where(iota((16, 128), 1) < 64, mine[:16, 128:], mine[16:, 128:])
        rs_out[c] = jnp.concatenate([mine[:, :128], tail], axis=0).astype(BF16)

    def send_rs(s, carry):
        to = lax.rem(k + s, colat)
        pltpu.make_async_remote_copy(
            src_ref=rs_out.at[to],
            dst_ref=rs_in.at[k],
            send_sem=rs_send,
            recv_sem=rs_recv,
            device_id={"colat": to},
            device_id_type=MESH,
        ).start()
        return carry

    lax.fori_loop(1, colat, send_rs, 0)
    keep_rs = pltpu.make_async_copy(rs_out.at[k], rs_in.at[k], local_sem.at[3])
    keep_rs.start()
    keep_rs.wait()
    pltpu.make_async_copy(rs_in.at[pl.ds(0, colat - 1)], rs_in.at[pl.ds(0, colat - 1)], rs_recv).wait()
    total = rs_in[0].astype(F32)
    for c in range(1, colat):
        total = total + rs_in[c].astype(F32)
    tail = jnp.concatenate([total[UC:, :], pltpu.roll(total[UC:, :], 64, 1)], axis=0)
    tail = jnp.where(iota((UC, 128), 1) < 64, tail, 0.0)
    g_hi, g_lo = split(jnp.concatenate([total[:UC, :], tail], axis=1))
    for r in range(4):
        gbd_hi[r * UC : (r + 1) * UC, r * 256 : (r + 1) * 256] = g_hi
        gbd_lo[r * UC : (r + 1) * UC, r * 256 : (r + 1) * 256] = g_lo
    outbox2[:, 0, :] = dot_nt(ohret[:, :1024], gbd_hi[...]) + dot_nt(ohret[:, :1024], gbd_lo[...])
    outbox2[:, 1, :] = dot_nt(ohret[:, 1024:], gbd_hi[:, :256]) + dot_nt(ohret[:, 1024:], gbd_lo[:, :256])

    def send_b(to):
        pltpu.make_async_remote_copy(
            src_ref=outbox2.at[to],
            dst_ref=inbox2.at[i],
            send_sem=b_send,
            recv_sem=b_recv,
            device_id={"lon": to},
            device_id_type=MESH,
        ).start()

    for_peers(send_b)
    keep_b = pltpu.make_async_copy(outbox2.at[i], inbox2.at[i], local_sem.at[4])
    keep_b.start()
    keep_b.wait()
    pltpu.make_async_copy(inbox2.at[pl.ds(0, lon - 1)], inbox2.at[pl.ds(0, lon - 1)], b_recv).wait()
    field = jnp.sum(inbox2[...], axis=0)
    result = jnp.concatenate([field[0:1, r * UC : (r + 1) * UC] for r in range(4)] + [field[1:2, :UC]], axis=0)
    out[:, 0, :] = jnp.where(iota((slots, UC), 0) < count[0], result, 0.0)

    for copy in halos:
        copy.wait_send()
    pltpu.make_async_copy(outbox.at[pl.ds(0, lon - 1)], outbox.at[pl.ds(0, lon - 1)], a_send).wait()
    pltpu.make_async_copy(rs_out.at[pl.ds(0, colat - 1)], rs_out.at[pl.ds(0, colat - 1)], rs_send).wait()
    pltpu.make_async_copy(outbox2.at[pl.ds(0, lon - 1)], outbox2.at[pl.ds(0, lon - 1)], b_send).wait()


def body(
    lon,
    colat,
    pattern,
    phi_filter,
    trans_table,
    partners,
    op_index,
    anter_weight,
    return_boxes,
    return_count,
    leaf_weight,
):
    nops, _, theta, _ = trans_table.shape
    npart, nbox = partners.shape[1], partners.shape[0]
    slots = return_boxes.shape[1]
    phi = phi_filter.shape[0]
    users = leaf_weight.shape[3]
    ops_pad = -(-nops // 128) * 128
    vmem, hbm = pl.BlockSpec(memory_space=pltpu.VMEM), pl.BlockSpec(memory_space=pl.ANY)
    return pl.pallas_call(
        functools.partial(kernel, lon, colat),
        out_shape=jax.ShapeDtypeStruct((slots, 1, users // colat), F32),
        in_specs=[hbm] * 6 + [pl.BlockSpec(memory_space=pltpu.HBM)] + [hbm] * 2,
        out_specs=vmem,
        scratch_shapes=[
            pltpu.VMEM((pattern.size // phi, phi), BF16),
            pltpu.VMEM((phi, phi), BF16),
            pltpu.VMEM((npart, nbox), I32),
            pltpu.VMEM((npart, nbox), I32),
            pltpu.VMEM(anter_weight.shape[::-1], F32),
            pltpu.VMEM(return_boxes.shape[::-1], I32),
            pltpu.SMEM((1,), I32),
            pltpu.VMEM((lon, 2, 128), F32),
            pltpu.VMEM((lon, 2, 128), F32),
            pltpu.VMEM((phi, 128), F32),
            pltpu.VMEM((ops_pad * 8, theta), F32),
            pltpu.VMEM((ops_pad, 8 * theta), BF16),
            pltpu.VMEM((ops_pad, 8 * theta), BF16),
            pltpu.VMEM((128, 2 * ops_pad), BF16),
            pltpu.VMEM((128, 256), BF16),
            pltpu.VMEM((256, 256), BF16),
            pltpu.VMEM((users, 384), BF16),
            pltpu.VMEM((npart, 256), I32),
            pltpu.VMEM((npart, 256), I32),
            pltpu.VMEM((128, 256), BF16),
            pltpu.VMEM((npart, 128, 256), F32),
            pltpu.VMEM((npart, 256, 256), BF16),
            pltpu.VMEM((2, 16, 16, users), BF16),
            pltpu.VMEM((2, 8, 16, users), BF16),
            pltpu.VMEM((2, 8, 16, users), BF16),
            pltpu.VMEM((3, 16, 128), F32),
            pltpu.VMEM((128, 256), F32),
            pltpu.VMEM((colat, RS_ROWS, 128), BF16),
            pltpu.VMEM((colat, RS_ROWS, 128), BF16),
            pltpu.VMEM((128, 1024), BF16),
            pltpu.VMEM((128, 1024), BF16),
            pltpu.VMEM((lon, slots * 256), BF16),
            pltpu.VMEM((lon, 2, 128), F32),
            pltpu.VMEM((lon, 2, 128), F32),
            pltpu.SemaphoreType.DMA((7,)),
            pltpu.SemaphoreType.DMA((5,)),
            pltpu.SemaphoreType.DMA((4,)),
            pltpu.SemaphoreType.DMA((4,)),
            pltpu.SemaphoreType.DMA,
            pltpu.SemaphoreType.DMA,
            pltpu.SemaphoreType.DMA,
            pltpu.SemaphoreType.DMA,
            pltpu.SemaphoreType.DMA,
            pltpu.SemaphoreType.DMA,
        ],
        compiler_params=pltpu.CompilerParams(
            collective_id=0, has_side_effects=True, vmem_limit_bytes=60 * 1024 * 1024
        ),
        name="mlfma_pass",
    )(
        pattern.reshape(-1, phi),
        phi_filter,
        partners.T,
        op_index.T,
        anter_weight.T,
        return_boxes.T,
        return_count,
        trans_table.transpose(0, 1, 3, 2).reshape(nops * 8, theta),
        leaf_weight,
    ).transpose(1, 0, 2)


def solution(mesh):
    in_specs = (
        P("lon", None, "colat", None),
        P(),
        P(None, None, None, "lon"),
        P(),
        P(),
        P(None, "colat"),
        P(),
        P("lon"),
        P(None, "colat", None, None),
    )
    out_specs = P("lon", None, "colat")
    run = functools.partial(body, mesh.shape["lon"], mesh.shape["colat"])
    return jax.shard_map(run, mesh=mesh, in_specs=in_specs, out_specs=out_specs, check_vma=False)
```
